512 devices in a mesh: row: 32 (over y, z_lo), col: 16 (over z_hi, x, core).
Axes of the slice: x: 4, y: 4, z: 16 (z_hi: 2, z_lo: 8; z = z_hi * 8 + z_lo), core: 2. Of those that a mesh axis runs over, the one named last changes fastest.
Arguments:
- inverse_block: bfloat16 [20480, 20480], P('row', 'col'), may hold values from -0.078125 to 0.078125
- lower_panel: bfloat16 [20480, 2, 384], P(('row', 'col')), may hold values from -0.75 to 0.75
- structure: int32 [160, 2], replicated, may hold values 0 or 1
- diag_inverse: float32 [2, 384, 384], P(None, 'row'), may hold values from -6 to 6
Outputs:
- inverse_panel: bfloat16 [20480, 2, 384], P(('row', 'col'))
- diag_block: float32 [2, 384, 384], P(None, 'row')
The draws below stay inside these ranges and needn't reach their ends.
Inputs may be any that keep to these rules, and one draw needn't show every extreme that they name: `structure`: 1 where the block of rows belongs to the panel.
All inputs are finite; a program needn't handle non-finite values.
Results may differ from the reference program's by a relative error of at most 0.013.
Values may be sent and summed in bfloat16 or wider, within the bound.
No kernel may reach another device: no remote copies, remote signals or barrier semaphores. Data moves between devices by JAX's collectives and lax.ppermute only.
A program may use at most 64 MiB of HBM per device.

```python
import jax
import jax.numpy as jnp
from jax import lax

M = 20480
W = 384
BS = 128
P_SIZE = 2
NB = 160
N_ROW = 32


def with_ends(entries, own_key, smallest, top_value):
    index_at = [jax.random.randint(jax.random.fold_in(own_key, axis), (), 0, length) for axis, length in enumerate(entries.shape)]
    main_axis = entries.shape.index(max(entries.shape))
    next_to = index_at[:main_axis] + [(index_at[main_axis] + 1) % entries.shape[main_axis]] + index_at[main_axis + 1:]
    return entries.at[tuple(index_at)].set(smallest).at[tuple(next_to)].set(top_value)


def block_scale(rng, dims, split, low, high):
    level, own = 1.0, jax.random.fold_in(rng, 6)
    for dim, shards_of in split:
        steps = jnp.exp(jax.random.uniform(jax.random.fold_in(own, dim), (shards_of,), jnp.float32, low / len(split), high / len(split)))
        level = level * jnp.repeat(steps, dims[dim] // shards_of).reshape([-1 if axis == dim else 1 for axis in range(len(dims))])
    return level


def noise(rng, extent, deviation, limit, shards=(), dtype=jnp.bfloat16):
    array = deviation * jax.random.normal(rng, extent, jnp.float32)
    if shards:
        array = array * block_scale(rng, extent, shards, -0.22, 0.18)
    return jnp.clip(array, -limit, limit).astype(dtype)


def setup_inputs(seed: int = 0) -> dict:
    splits = jax.random.split(jax.random.key(seed), 5)
    return {
        "inverse_block": noise(splits[0], (M, M), (M // 4) ** -0.5, 0.078125, ((0, 32), (1, 16))),
        "lower_panel": noise(splits[1], (M, P_SIZE, W), 0.12, 0.75, ((0, 512),)),
        "structure": with_ends((jax.random.randint(splits[2], (NB, P_SIZE), 0, 2) < 1).astype(jnp.int32), jax.random.fold_in(splits[2], 1), 0, 1),
        "diag_inverse": noise(splits[3], (P_SIZE, W, W), 1.0, 6.0, ((1, 32),), jnp.float32),
    }


def reference(inverse_block, lower_panel, structure, diag_inverse):
    keep_rows = jnp.repeat(structure, BS, axis=0)
    masked = lower_panel * keep_rows[:, :, None].astype(jnp.bfloat16)
    flat_panel = masked.reshape(M, P_SIZE * W).astype(jnp.float32)

    def row_product(block_rows):
        return jnp.dot(block_rows.astype(jnp.float32), flat_panel, precision=lax.Precision.HIGHEST)

    product = lax.map(row_product, inverse_block.reshape(N_ROW, M // N_ROW, M)).reshape(M, P_SIZE, W)
    inverse_panel = (-product).astype(jnp.bfloat16)
    schur_term = jnp.einsum("rpi,rpj->pij", masked.astype(jnp.float32), product, precision=lax.Precision.HIGHEST)
    return inverse_panel, diag_inverse + schur_term
```

```python
import jax
import jax.numpy as jnp
from jax import lax
from jax.sharding import Mesh, PartitionSpec as P

BS = 128
AXES = ("y", "g", "q", "zh", "x", "k")
SIZES = (4, 2, 4, 2, 4, 2)
ROW = ("y", "g", "q")
COL = ("zh", "x", "k")


def swapped(x, axis):
    return lax.ppermute(x, axis, [(0, 1), (1, 0)])


def to_columns():
    route = []
    for row in range(32):
        for col in range(16):
            zh, x, k = col // 8, (col // 2) % 4, col % 2
            target_row = ((row % 2) * 2 + zh) * 8 + k * 4 + x
            route.append((row * 16 + col, target_row * 16 + row // 2))
    return route


def gathered(x, axis):
    n = lax.axis_size(axis)
    return lax.all_to_all(jnp.broadcast_to(x[None], (n,) + x.shape), axis, 0, 0)


def ordered(mine, other, index):
    first = jnp.where(index == 0, mine, other)
    second = jnp.where(index == 0, other, mine)
    return jnp.stack([first, second])


def masked_rows(lower_panel, structure):
    rows = lower_panel.shape[0]
    start = (lax.axis_index(ROW) * 16 + lax.axis_index(COL)) * rows
    block_ids = (start + lax.iota(jnp.int32, rows)) // BS
    onehot = (block_ids[:, None] == lax.iota(jnp.int32, structure.shape[0])[None, :]).astype(jnp.float32)
    keep = jnp.dot(onehot, structure.astype(jnp.float32))
    return lower_panel * keep[:, :, None].astype(jnp.bfloat16)


def added(parts):
    return jnp.sum(parts.astype(jnp.float32), axis=0)


def shards(inverse_block, lower_panel, structure, diag_inverse):
    f32, bf16 = jnp.float32, jnp.bfloat16
    k = lax.axis_index("k")
    zh = lax.axis_index("zh")
    flat = masked_rows(lower_panel, structure).reshape(40, 768)

    pair = ordered(flat, swapped(flat, "k"), k)
    moved = lax.ppermute(pair, AXES, to_columns())
    quarter = gathered(moved.reshape(80, 768), "q").reshape(320, 768)
    own_rows = jnp.where(k == 0, pair[..., :384], pair[..., 384:])
    quarter, own_rows = lax.optimization_barrier((quarter, own_rows))
    columns = gathered(quarter, "y").reshape(1280, 768)
    far_rows = swapped(own_rows, "zh")
    columns, far_rows = lax.optimization_barrier((columns, far_rows))

    product = jnp.dot(inverse_block, columns, preferred_element_type=f32)

    mine = jnp.where(k == 0, product[:, :384], product[:, 384:])
    sent = jnp.where(k == 0, product[:, 384:], product[:, :384]).astype(bf16)
    summed = (mine + swapped(sent, "k").astype(f32)).astype(bf16)
    chunks = summed.reshape(2, 4, 80, 384).transpose(1, 0, 2, 3)
    near = added(lax.all_to_all(chunks, "x", 0, 0))
    near_b = near.astype(bf16)

    rows = ordered(own_rows, far_rows, zh).reshape(160, 384)
    schur = lax.dot_general(
        rows, near_b.reshape(160, 384), (((0,), (0,)), ((), ())), preferred_element_type=f32
    ).astype(bf16)

    by_yq = schur.reshape(4, 2, 4, 12, 384).transpose(0, 2, 1, 3, 4)
    by_yq = added(lax.all_to_all(by_yq.reshape(16, 2, 12, 384), ("y", "q"), 0, 0)).astype(bf16)

    near_b = near_b.reshape(2, 2, 40, 384)
    kept = jnp.where(k == 0, near_b[:, 0], near_b[:, 1])
    other = swapped(jnp.where(k == 0, near_b[:, 1], near_b[:, 0]), "k")
    halves = jnp.stack([jnp.where(k == 0, kept, other), jnp.where(k == 0, other, kept)], axis=1)
    halves, by_yq = lax.optimization_barrier((halves, by_yq))
    by_z = jnp.broadcast_to(by_yq[:, None], (2, 2, 12, 384)).reshape(4, 12, 384)
    by_z = added(lax.all_to_all(by_z, ("g", "zh"), 0, 0)).astype(bf16)
    far_half = swapped(jnp.where(zh == 0, halves[1], halves[0]), "zh").astype(f32)
    own_half = jnp.where(zh == 0, halves[0], halves[1]).astype(f32)
    inverse_panel = (-(own_half + far_half)).astype(bf16).transpose(1, 0, 2)

    total = jnp.sum(gathered(by_z, ("x", "k")).reshape(4, 2, 12, 384).astype(f32), axis=0)
    return inverse_panel, diag_inverse + total


def solution(mesh):
    fine = Mesh(mesh.devices.reshape(SIZES), AXES)
    return jax.shard_map(
        shards,
        mesh=fine,
        in_specs=(P(ROW, COL), P(AXES, None, None), P(), P(None, ROW, None)),
        out_specs=(P(AXES, None, None), P(None, ROW, None)),
        check_vma=False,
    )
```

```python
import jax
import jax.numpy as jnp
from jax import lax
from jax.sharding import Mesh, PartitionSpec as P

BS = 128
LATE = True
AXES = ("y", "g", "q", "zh", "x", "k")
SIZES = (4, 2, 4, 2, 4, 2)
ROW = ("y", "g", "q")
COL = ("zh", "x", "k")


def swapped(x, axis):
    return lax.ppermute(x, axis, [(0, 1), (1, 0)])


def to_columns():
    route = []
    for row in range(32):
        for col in range(16):
            zh, x, k = col // 8, (col // 2) % 4, col % 2
            target_row = ((row % 2) * 2 + zh) * 8 + k * 4 + x
            route.append((row * 16 + col, target_row * 16 + row // 2))
    return route


def gathered(x, axis):
    n = lax.axis_size(axis)
    return lax.all_to_all(jnp.broadcast_to(x[None], (n,) + x.shape), axis, 0, 0)


def ordered(mine, other, index):
    first = jnp.where(index == 0, mine, other)
    second = jnp.where(index == 0, other, mine)
    return jnp.stack([first, second])


def masked_pair(lower_panel, structure, k):
    rows = lower_panel.shape[0]
    flat = lower_panel.reshape(rows, 768)
    pair = ordered(flat, swapped(flat, "k"), k)
    start = (lax.axis_index(ROW) * 16 + lax.axis_index(COL) - k) * rows
    block = start // BS
    here = lax.dynamic_slice_in_dim(structure, block, 1, 0)
    after_it = lax.dynamic_slice_in_dim(structure, jnp.minimum(block + 1, structure.shape[0] - 1), 1, 0)
    row = start + lax.broadcasted_iota(jnp.int32, (2 * rows, 1), 0)
    keep = jnp.where(row < (block + 1) * BS, here, after_it).astype(jnp.bfloat16)
    keep = jnp.repeat(keep, 384, axis=1).reshape(2, rows, 768)
    return pair * keep


def added(parts):
    return jnp.sum(parts.astype(jnp.float32), axis=0)


def after(x, first):
    return lax.optimization_barrier((x, first))[0]


def turned(x, axis, d):
    n = lax.axis_size(axis)
    return lax.ppermute(x, axis, [(i, (i + d) % n) for i in range(n)])


def ring_of_four(x, axis):
    half = x.shape[0] // 2
    up, down = turned(x, axis, 1), turned(x, axis, 3)
    across = jnp.concatenate([turned(up[:half], axis, 1), turned(down[half:], axis, 3)])
    i = lax.axis_index(axis)
    by_distance = jnp.stack([x, up, across, down])
    order = [lax.dynamic_index_in_dim(by_distance, (i - j) % 4, 0, keepdims=False) for j in range(4)]
    return jnp.concatenate(order)


def piece(chunks, i):
    return lax.dynamic_index_in_dim(chunks, i, 1, keepdims=False)


def in_order(by_distance, x):
    return jnp.stack([lax.dynamic_index_in_dim(by_distance, (x - j) % 4, 1, keepdims=False) for j in range(4)], axis=1)


def panel(x, p):
    return x[..., p * 384 : (p + 1) * 384]


def shards(inverse_block, lower_panel, structure, diag_inverse):
    f32, bf16 = jnp.float32, jnp.bfloat16
    k = lax.axis_index("k")
    zh = lax.axis_index("zh")
    pair = masked_pair(lower_panel, structure, k)
    own_rows = jnp.where(k == 0, panel(pair, 0), panel(pair, 1))
    moved = lax.ppermute(pair, AXES, to_columns())
    quarter = lax.all_gather(moved.reshape(80, 768), "q", tiled=True)
    own_rows = after(own_rows, quarter)
    far_rows = swapped(own_rows, "zh")
    near_rows = ordered(own_rows, far_rows, zh)
    columns = ring_of_four(quarter, "y")
    by_distance = [near_rows] + [turned(near_rows, "x", d) for d in (1, 3, 2)]
    by_distance = jnp.stack([by_distance[j] for j in (0, 1, 3, 2)], axis=1)
    product = jnp.dot(inverse_block, columns, preferred_element_type=f32)
    products = [panel(product, p) for p in range(2)]

    mine = jnp.where(k == 0, products[0], products[1])
    sent = jnp.where(k == 0, products[1], products[0]).astype(bf16)
    summed = (mine + swapped(sent, "k").astype(f32)).astype(bf16)

    x = lax.axis_index("x")
    chunks = summed.reshape(2, 4, 80, 384)
    all_rows = in_order(by_distance, x).reshape(640, 384)
    schur = lax.dot_general(
        all_rows, summed, (((0,), (0,)), ((), ())), preferred_element_type=f32
    ).astype(bf16)
    by_yq = schur.reshape(4, 2, 4, 12, 384).transpose(0, 2, 1, 3, 4)
    by_yq = added(lax.all_to_all(by_yq.reshape(16, 2, 12, 384), ("y", "q"), 0, 0)).astype(bf16)

    if LATE:
        chunks = after(chunks, schur)
    parts = [piece(chunks, x)] + [turned(piece(chunks, (x + d) % 4), "x", d) for d in (1, 3, 2)]
    parts, _ = lax.optimization_barrier((parts, by_yq))
    near = added(jnp.stack(parts))
    near = near.astype(bf16).reshape(2, 2, 40, 384)

    kept = jnp.where(k == 0, near[:, 0], near[:, 1])
    other = swapped(jnp.where(k == 0, near[:, 1], near[:, 0]), "k")
    halves = jnp.stack([jnp.where(k == 0, kept, other), jnp.where(k == 0, other, kept)], axis=1)
    halves = after(halves, by_yq)
    by_z = jnp.broadcast_to(by_yq[:, None], (2, 2, 12, 384)).reshape(4, 12, 384)
    by_z = added(lax.all_to_all(by_z, ("g", "zh"), 0, 0)).astype(bf16)
    far_half = swapped(jnp.where(zh == 0, halves[1], halves[0]), "zh").astype(f32)
    own_half = jnp.where(zh == 0, halves[0], halves[1]).astype(f32)
    inverse_panel = (-(own_half + far_half)).astype(bf16).transpose(1, 0, 2)

    total = jnp.sum(gathered(by_z, ("x", "k")).reshape(4, 2, 12, 384).astype(f32), axis=0)
    return inverse_panel, diag_inverse + total


def solution(mesh):
    fine = Mesh(mesh.devices.reshape(SIZES), AXES)
    return jax.shard_map(
        shards,
        mesh=fine,
        in_specs=(P(ROW, COL), P(AXES, None, None), P(), P(None, ROW, None)),
        out_specs=(P(AXES, None, None), P(None, ROW, None)),
        check_vma=False,
    )
```

```python
import jax
import jax.numpy as jnp
from jax import lax
from jax.sharding import Mesh, PartitionSpec as P

BS = 128

AXES = ("y", "g", "q", "zh", "x", "k")
SIZES = (4, 2, 4, 2, 4, 2)
ROW = ("y", "g", "q")
COL = ("zh", "x", "k")

def swapped(x, axis):
    return lax.ppermute(x, axis, [(0, 1), (1, 0)])

def to_columns():
    route = []
    for row in range(32):
        for col in range(16):
            zh, x, k = col // 8, (col // 2) % 4, col % 2
            target_row = ((row % 2) * 2 + zh) * 8 + k * 4 + x
            route.append((row * 16 + col, target_row * 16 + row // 2))
    return route

def gathered(x, axis):
    n = lax.axis_size(axis)
    return lax.all_to_all(jnp.broadcast_to(x[None], (n,) + x.shape), axis, 0, 0)

def ordered(mine, other, index):
    first = jnp.where(index == 0, mine, other)
    second = jnp.where(index == 0, other, mine)
    return jnp.stack([first, second])

def masked_pair(lower_panel, structure, k):
    rows = lower_panel.shape[0]
    flat = lower_panel.reshape(rows, 768)
    pair = ordered(flat, swapped(flat, "k"), k)
    start = (lax.axis_index(ROW) * 16 + lax.axis_index(COL) - k) * rows
    block = start // BS
    here = lax.dynamic_slice_in_dim(structure, block, 1, 0)
    after_it = lax.dynamic_slice_in_dim(structure, jnp.minimum(block + 1, structure.shape[0] - 1), 1, 0)
    row = start + lax.broadcasted_iota(jnp.int32, (2 * rows, 1), 0)
    keep = jnp.where(row < (block + 1) * BS, here, after_it).astype(jnp.bfloat16)
    keep = jnp.repeat(keep, 384, axis=1).reshape(2, rows, 768)
    return pair * keep

def added(parts):
    return jnp.sum(parts.astype(jnp.float32), axis=0)

def after(x, first):
    return lax.optimization_barrier((x, first))[0]

def turned(x, axis, d):
    n = lax.axis_size(axis)
    return lax.ppermute(x, axis, [(i, (i + d) % n) for i in range(n)])

def ring_of_four(x, axis):
    half = x.shape[0] // 2
    up, down = turned(x, axis, 1), turned(x, axis, 3)
    across = jnp.concatenate([turned(up[:half], axis, 1), turned(down[half:], axis, 3)])
    i = lax.axis_index(axis)
    by_distance = jnp.stack([x, up, across, down])
    order = [lax.dynamic_index_in_dim(by_distance, (i - j) % 4, 0, keepdims=False) for j in range(4)]
    return jnp.concatenate(order)

def piece(chunks, i):
    return lax.dynamic_index_in_dim(chunks, i, 1, keepdims=False)

def in_order(by_distance, x):
    return jnp.stack([lax.dynamic_index_in_dim(by_distance, (x - j) % 4, 1, keepdims=False) for j in range(4)], axis=1)

def panel(x, p):
    return x[..., p * 384 : (p + 1) * 384]

def shards(inverse_block, lower_panel, structure, diag_inverse):
    f32, bf16 = jnp.float32, jnp.bfloat16
    k = lax.axis_index("k")
    zh = lax.axis_index("zh")
    pair = masked_pair(lower_panel, structure, k)
    own_rows = jnp.where(k == 0, panel(pair, 0), panel(pair, 1))
    moved = lax.ppermute(pair, AXES, to_columns())
    moved = jnp.where(k == 0, moved, jnp.concatenate([panel(moved, 1), panel(moved, 0)], axis=-1))
    quarter = lax.all_gather(moved.reshape(80, 768), "q", tiled=True)
    far_rows = swapped(own_rows, "zh")
    near_rows = ordered(own_rows, far_rows, zh)
    columns = ring_of_four(quarter, "y")
    own_columns, other_columns = panel(columns, 0), panel(columns, 1)
    by_distance = [near_rows] + [turned(near_rows, "x", d) for d in (1, 3, 2)]
    by_distance = jnp.stack([by_distance[j] for j in (0, 1, 3, 2)], axis=1)

    sent = jnp.dot(inverse_block, other_columns, preferred_element_type=f32).astype(bf16)
    arrived = swapped(sent, "k")
    summed = (jnp.dot(inverse_block, own_columns, preferred_element_type=f32) + arrived.astype(f32)).astype(bf16)

    x = lax.axis_index("x")
    chunks = summed.reshape(2, 4, 80, 384)
    all_rows = in_order(by_distance, x).reshape(640, 384)
    schur = lax.dot_general(
        all_rows, summed, (((0,), (0,)), ((), ())), preferred_element_type=f32
    ).astype(bf16)
    by_yq = schur.reshape(4, 2, 4, 12, 384).transpose(0, 2, 1, 3, 4)
    by_yq = added(lax.all_to_all(by_yq.reshape(16, 2, 12, 384), ("y", "q"), 0, 0)).astype(bf16)

    chunks = after(chunks, schur)
    parts = [piece(chunks, x)] + [turned(piece(chunks, (x + d) % 4), "x", d) for d in (1, 3, 2)]
    parts, _ = lax.optimization_barrier((parts, by_yq))
    near = added(jnp.stack(parts))
    near = near.astype(bf16).reshape(2, 2, 40, 384)

    kept = jnp.where(k == 0, near[:, 0], near[:, 1])
    other = swapped(jnp.where(k == 0, near[:, 1], near[:, 0]), "k")
    halves = jnp.stack([jnp.where(k == 0, kept, other), jnp.where(k == 0, other, kept)], axis=1)
    halves = after(halves, by_yq)
    by_z = jnp.broadcast_to(by_yq[:, None], (2, 2, 12, 384)).reshape(4, 12, 384)
    by_z = added(lax.all_to_all(by_z, ("g", "zh"), 0, 0)).astype(bf16)
    far_half = swapped(jnp.where(zh == 0, halves[1], halves[0]), "zh").astype(f32)
    own_half = jnp.where(zh == 0, halves[0], halves[1]).astype(f32)
    inverse_panel = (-(own_half + far_half)).astype(bf16).transpose(1, 0, 2)

    total = jnp.sum(gathered(by_z, ("x", "k")).reshape(4, 2, 12, 384).astype(f32), axis=0)
    return inverse_panel, diag_inverse + total

def solution(mesh):
    fine = Mesh(mesh.devices.reshape(SIZES), AXES)
    return jax.shard_map(
        shards,
        mesh=fine,
        in_specs=(P(ROW, COL), P(AXES, None, None), P(), P(None, ROW, None)),
        out_specs=(P(AXES, None, None), P(None, ROW, None)),
        check_vma=False,
    )
```

```python
import jax
import jax.numpy as jnp
from jax import lax
from jax.sharding import Mesh, PartitionSpec as P

BS = 128

AXES = ("y", "g", "q", "zh", "x", "k")
SIZES = (4, 2, 4, 2, 4, 2)
ROW = ("y", "g", "q")
COL = ("zh", "x", "k")

def swapped(x, axis):
    return lax.ppermute(x, axis, [(0, 1), (1, 0)])

def to_columns():
    route = []
    for row in range(32):
        for col in range(16):
            zh, x, k = col // 8, (col // 2) % 4, col % 2
            target_row = ((row % 2) * 2 + zh) * 8 + k * 4 + x
            route.append((row * 16 + col, target_row * 16 + row // 2))
    return route

def gathered(x, axis):
    n = lax.axis_size(axis)
    return lax.all_to_all(jnp.broadcast_to(x[None], (n,) + x.shape), axis, 0, 0)

def ordered(mine, other, index):
    first = jnp.where(index == 0, mine, other)
    second = jnp.where(index == 0, other, mine)
    return jnp.stack([first, second])

def masked_pair(lower_panel, structure, k):
    rows = lower_panel.shape[0]
    pair = ordered(lower_panel, swapped(lower_panel, "k"), k)
    start = (lax.axis_index(ROW) * 16 + lax.axis_index(COL) - k) * rows
    block = start // BS
    here = lax.dynamic_slice_in_dim(structure, block, 1, 0)
    after_it = lax.dynamic_slice_in_dim(structure, jnp.minimum(block + 1, structure.shape[0] - 1), 1, 0)
    row = start + lax.broadcasted_iota(jnp.int32, (2 * rows, 1), 0)
    keep = jnp.where(row < (block + 1) * BS, here, after_it).astype(jnp.bfloat16)
    return (pair * keep.reshape(2, rows, 2, 1)).reshape(2, rows, 768)

def added(parts):
    return jnp.sum(parts.astype(jnp.float32), axis=0)

def after(x, first):
    return lax.optimization_barrier((x, first))[0]

def turned(x, axis, d):
    n = lax.axis_size(axis)
    return lax.ppermute(x, axis, [(i, (i + d) % n) for i in range(n)])

def ring_of_four(x, axis):
    half = x.shape[0] // 2
    up, down = turned(x, axis, 1), turned(x, axis, 3)
    across = jnp.concatenate([turned(up[:half], axis, 1), turned(down[half:], axis, 3)])
    i = lax.axis_index(axis)
    by_distance = jnp.stack([x, up, across, down])
    order = [lax.dynamic_index_in_dim(by_distance, (i - j) % 4, 0, keepdims=False) for j in range(4)]
    return jnp.concatenate(order)

def piece(chunks, i):
    return lax.dynamic_index_in_dim(chunks, i, 1, keepdims=False)

def in_order(by_distance, x):
    return jnp.stack([lax.dynamic_index_in_dim(by_distance, (x - j) % 4, 1, keepdims=False) for j in range(4)], axis=1)

def panel(x, p):
    return x[..., p * 384 : (p + 1) * 384]

def shards(inverse_block, lower_panel, structure, diag_inverse):
    f32, bf16 = jnp.float32, jnp.bfloat16
    k = lax.axis_index("k")
    zh = lax.axis_index("zh")
    pair = masked_pair(lower_panel, structure, k)
    own_rows = jnp.where(k == 0, panel(pair, 0), panel(pair, 1))
    moved = lax.ppermute(pair, AXES, to_columns())
    moved = jnp.where(k == 0, moved, jnp.concatenate([panel(moved, 1), panel(moved, 0)], axis=-1))
    quarter = lax.all_gather(moved.reshape(80, 768), "q", tiled=True)
    far_rows = swapped(own_rows, "zh")
    near_rows = ordered(own_rows, far_rows, zh)
    columns = ring_of_four(quarter, "y")
    own_columns, other_columns = panel(columns, 0), panel(columns, 1)
    by_distance = [near_rows] + [turned(near_rows, "x", d) for d in (1, 3, 2)]
    by_distance = jnp.stack([by_distance[j] for j in (0, 1, 3, 2)], axis=1)

    sent = jnp.dot(inverse_block, other_columns, preferred_element_type=f32).astype(bf16)
    arrived = swapped(sent, "k")
    summed = (jnp.dot(inverse_block, own_columns, preferred_element_type=f32) + arrived.astype(f32)).astype(bf16)

    x = lax.axis_index("x")
    chunks = summed.reshape(2, 4, 80, 384)
    all_rows = in_order(by_distance, x).reshape(640, 384)
    schur = lax.dot_general(
        all_rows, summed, (((0,), (0,)), ((), ())), preferred_element_type=f32
    ).astype(bf16)
    by_yq = schur.reshape(4, 2, 4, 12, 384).transpose(0, 2, 1, 3, 4)
    by_yq = added(lax.all_to_all(by_yq.reshape(16, 2, 12, 384), ("y", "q"), 0, 0)).astype(bf16)

    chunks = after(chunks, schur)
    parts = [piece(chunks, x)] + [turned(piece(chunks, (x + d) % 4), "x", d) for d in (1, 3, 2)]
    parts, _ = lax.optimization_barrier((parts, by_yq))
    near = added(jnp.stack(parts))
    near = near.astype(bf16).reshape(2, 2, 40, 384)

    kept = jnp.where(k == 0, near[:, 0], near[:, 1])
    other = swapped(jnp.where(k == 0, near[:, 1], near[:, 0]), "k")
    halves = jnp.stack([jnp.where(k == 0, kept, other), jnp.where(k == 0, other, kept)], axis=1)
    halves = after(halves, by_yq)
    by_z = jnp.broadcast_to(by_yq[:, None], (2, 2, 12, 384)).reshape(4, 12, 384)
    by_z = added(lax.all_to_all(by_z, ("g", "zh"), 0, 0)).astype(bf16)
    far_half = swapped(jnp.where(zh == 0, halves[1], halves[0]), "zh").astype(f32)
    own_half = jnp.where(zh == 0, halves[0], halves[1]).astype(f32)
    inverse_panel = (-(own_half + far_half)).astype(bf16).transpose(1, 0, 2)

    total = jnp.sum(gathered(by_z, ("x", "k")).reshape(4, 2, 12, 384).astype(f32), axis=0)
    return inverse_panel, diag_inverse + total

def solution(mesh):
    fine = Mesh(mesh.devices.reshape(SIZES), AXES)
    return jax.shard_map(
        shards,
        mesh=fine,
        in_specs=(P(ROW, COL), P(AXES, None, None), P(), P(None, ROW, None)),
        out_specs=(P(AXES, None, None), P(None, ROW, None)),
        check_vma=False,
    )
```
